768 devices in a mesh: replica: 96 (over x, y, z_lo), fsdp: 8 (over z_hi, core).
Axes of the slice: x: 4, y: 8, z: 12 (z_hi: 4, z_lo: 3; z = z_hi * 3 + z_lo), core: 2. Of those that a mesh axis runs over, the one named last changes fastest.
Arguments:
- weights: bfloat16 [96, 4096, 512], P('replica', 'fsdp'), may hold values from -6 to 6
- pseudo_grad: bfloat16 [96, 4096, 512], P('replica', 'fsdp'), may hold values from -6 to 6
- momentum: bfloat16 [96, 4096, 512], P('replica', 'fsdp'), may hold values from -6 to 6
- partner: int32 [96], replicated, may hold values from 0 to 95, as said below
- activations: bfloat16 [98304, 4096], P('replica', 'fsdp'), may hold values from -6 to 6
- key_cotangent: bfloat16 [98304, 512], P(('replica', 'fsdp')), may hold values from -0.1875 to 0.1875
Outputs:
- new_weights: bfloat16 [96, 4096, 512], P('replica', 'fsdp')
- new_momentum: bfloat16 [96, 4096, 512], P('replica', 'fsdp')
- weight_grad: bfloat16 [96, 4096, 512], P('replica', 'fsdp')
The draws below stay inside these ranges and needn't reach their ends.
Inputs may be any that keep to these rules, and one draw needn't show every extreme that they name: partner is a matching: partner[partner[r]] = r and partner[r] != r for every replica r.
All inputs are finite; a program needn't handle non-finite values.
Results may differ from the reference program's by a relative error of at most 0.001.
Values may be sent and summed in bfloat16 or wider, within the bound.
No kernel may reach another device: no remote copies, remote signals or barrier semaphores. Data moves between devices by JAX's collectives and lax.ppermute only.
A program may use at most 32 MiB of HBM per device.

```python
import jax
import jax.numpy as jnp
from jax import lax

D = 4096
KW = 512
TOK_REP = 1024
TOKENS = 98304
N_REPLICA = 96


def draw_partner(key, part):
    key = jax.random.fold_in(key, 11)
    order = jax.random.permutation(key, N_REPLICA).astype(jnp.int32)
    first_half = order[0::2]
    second_half = order[1::2]
    matched = jnp.zeros((N_REPLICA,), jnp.int32)
    matched = matched.at[first_half].set(second_half)
    matched = matched.at[second_half].set(first_half)
    return matched


def levels(own_key, dims, pieces, least, top_value):
    factor_of, own = 1.0, jax.random.fold_in(own_key, 6)
    for axis_at, blocks in pieces:
        heights = jnp.exp(jax.random.uniform(jax.random.fold_in(own, axis_at), (blocks,), jnp.float32, least / len(pieces), top_value / len(pieces)))
        factor_of = factor_of * jnp.repeat(heights, dims[axis_at] // blocks).reshape([-1 if axis == axis_at else 1 for axis in range(len(dims))])
    return factor_of


def normal_values(key, extent, width, limit, shards=(), dtype=jnp.bfloat16):
    values = width * jax.random.normal(key, extent, jnp.float32)
    if shards:
        values = values * levels(key, extent, shards, -0.22, 0.18)
    return jnp.clip(values, -limit, limit).astype(dtype)


def setup_inputs(seed: int = 0) -> dict:
    keys = jax.random.split(jax.random.key(seed), 7)
    return {
        "weights": normal_values(keys[0], (N_REPLICA, D, KW), 1.0, 6.0, ((0, 96), (1, 8))),
        "pseudo_grad": normal_values(keys[1], (N_REPLICA, D, KW), 1.0, 6.0, ((0, 96), (1, 8))),
        "momentum": normal_values(keys[2], (N_REPLICA, D, KW), 1.0, 6.0, ((0, 96), (1, 8))),
        "partner": draw_partner(jax.random.fold_in(keys[6], 71), 0),
        "activations": normal_values(keys[4], (TOKENS, D), 1.0, 6.0, ((0, 96), (1, 8))),
        "key_cotangent": normal_values(keys[5], (TOKENS, KW), (TOK_REP ** -0.5), 0.1875, ((0, 768),)),
    }


decay_old = 0.5
grad_rate = 0.7
pull_rate = 0.9

def replica_grad(operands):
    inputs_rep, cotan_rep = operands
    return lax.dot_general(inputs_rep, cotan_rep, (((0,), (0,)), ((), ())), preferred_element_type=jnp.float32).astype(jnp.bfloat16)

def reference(weights, pseudo_grad, momentum, partner, activations, key_cotangent):
    partner_weights = jnp.take(weights, partner, axis=0)
    partner_grad = jnp.take(pseudo_grad, partner, axis=0)
    weights_f32 = weights.astype(jnp.float32)
    mean_weights = (weights_f32 + partner_weights.astype(jnp.float32)) * 0.5
    mean_grad = (pseudo_grad.astype(jnp.float32) + partner_grad.astype(jnp.float32)) * 0.5
    momentum_f = decay_old * momentum.astype(jnp.float32) - grad_rate * mean_grad - pull_rate * (weights_f32 - mean_weights)
    new_weights = (weights_f32 + decay_old * momentum_f - grad_rate * mean_grad).astype(jnp.bfloat16)
    new_momentum = momentum_f.astype(jnp.bfloat16)
    inputs_all = activations.reshape(N_REPLICA, TOK_REP, D)
    cotan_all = key_cotangent.reshape(N_REPLICA, TOK_REP, KW)
    weight_grad = lax.map(replica_grad, (inputs_all, cotan_all))
    return (new_weights, new_momentum, weight_grad)
```

```python
import jax
import jax.numpy as jnp
from jax import lax
from jax.sharding import Mesh
from jax.sharding import PartitionSpec as P

LAYERS = 3
SLOTS = 18

decay_old = 0.5
grad_rate = 0.7
pull_rate = 0.9


def outer_step(weights, pseudo_grad, momentum, partner_weights, partner_grad):
    weights_f32 = weights.astype(jnp.float32)
    mean_weights = (weights_f32 + partner_weights.astype(jnp.float32)) * 0.5
    mean_grad = (pseudo_grad.astype(jnp.float32) + partner_grad.astype(jnp.float32)) * 0.5
    momentum_f = (
        decay_old * momentum.astype(jnp.float32)
        - grad_rate * mean_grad
        - pull_rate * (weights_f32 - mean_weights)
    )
    new_weights = weights_f32 + decay_old * momentum_f - grad_rate * mean_grad
    return new_weights.astype(jnp.bfloat16), momentum_f.astype(jnp.bfloat16)


def spread(array):
    columns = lax.axis_size("column")
    pieces = array.reshape(columns, array.shape[0] // columns, array.shape[1])
    return lax.all_to_all(pieces, "column", split_axis=0, concat_axis=0, tiled=True)


def deliver(pieces, send_index, take_index):
    crossed = lax.all_to_all(
        jnp.take(pieces, send_index, axis=0), "layer", split_axis=0, concat_axis=0, tiled=True
    )
    routed = jnp.take(crossed, take_index, axis=0)
    arrived = lax.all_to_all(routed, "column", split_axis=0, concat_axis=0, tiled=True)
    return arrived.reshape(-1, arrived.shape[-1])


def routes(target, rank, layer, slots):
    columns = target.shape[0]
    mine_to = jnp.take(target % LAYERS, layer, axis=1)
    mine_rank = jnp.take(rank, layer, axis=1)
    slot = mine_to * slots + mine_rank
    chosen = slot[None, :] == jnp.arange(LAYERS * slots, dtype=jnp.int32)[:, None]
    chosen = chosen & (mine_rank < slots)[None, :]
    send_index = jnp.sum(
        jnp.where(chosen, jnp.arange(columns, dtype=jnp.int32)[None, :], 0), axis=1
    )
    source = jnp.take(target, layer, axis=1)
    source_rank = jnp.take(rank.reshape(-1), source, axis=0)
    take_index = jnp.minimum(source % LAYERS * slots + source_rank, LAYERS * slots - 1)
    return send_index, take_index


def on_device(weights, pseudo_grad, momentum, partner, activations, key_cotangent):
    columns = lax.axis_size("column")
    layer = lax.axis_index("layer")
    weights, pseudo_grad, momentum = weights[0], pseudo_grad[0], momentum[0]

    target = partner.reshape(columns, LAYERS)
    to_layer = (target % LAYERS)[:, :, None] == jnp.arange(LAYERS, dtype=jnp.int32)
    before = jnp.tril(jnp.ones((columns, columns), jnp.int32), -1)
    earlier = jnp.sum(before[:, :, None, None] * to_layer[None].astype(jnp.int32), axis=1)
    rank = jnp.sum(jnp.where(to_layer, earlier, 0), axis=2)
    crowded = jnp.max(rank) >= SLOTS

    spread_weights = spread(weights)
    spread_grad = spread(pseudo_grad)
    send_index, take_index = routes(target, rank, layer, SLOTS)
    partner_weights = deliver(spread_weights, send_index, take_index)
    partner_grad = deliver(spread_grad, send_index, take_index)

    def as_arrived():
        return outer_step(weights, pseudo_grad, momentum, partner_weights, partner_grad)

    def again():
        index = routes(target, rank, layer, columns)
        return outer_step(
            weights,
            pseudo_grad,
            momentum,
            deliver(spread_weights, *index),
            deliver(spread_grad, *index),
        )

    new_weights, new_momentum = lax.cond(crowded, again, as_arrived)

    contract = (((0,), (0,)), ((), ()))
    gathered = lax.all_gather(key_cotangent, "fsdp", axis=0, tiled=True)
    grad_f32 = lax.dot_general(activations, gathered, contract, preferred_element_type=jnp.float32)
    weight_grad = grad_f32.astype(jnp.bfloat16)
    return (new_weights[None], new_momentum[None], weight_grad[None])


def solution(mesh):
    replicas, shards = mesh.devices.shape
    grid = Mesh(
        mesh.devices.reshape(replicas // LAYERS, LAYERS, shards), ("column", "layer", "fsdp")
    )
    replica = ("column", "layer")
    block = P(replica, "fsdp", None)
    return jax.shard_map(
        on_device,
        mesh=grid,
        in_specs=(
            block,
            block,
            block,
            P(),
            P(replica, "fsdp"),
            P(("column", "layer", "fsdp"), None),
        ),
        out_specs=(block, block, block),
        check_vma=False,
    )
```

```python
import jax
import jax.numpy as jnp
from jax import lax
from jax.sharding import Mesh
from jax.sharding import PartitionSpec as P

LAYERS = 3
SLOTS = 16

decay_old = 0.5
grad_rate = 0.7
pull_rate = 0.9


def outer_step(weights, pseudo_grad, momentum, partner_weights, partner_grad):
    weights_f32 = weights.astype(jnp.float32)
    mean_weights = (weights_f32 + partner_weights.astype(jnp.float32)) * 0.5
    mean_grad = (pseudo_grad.astype(jnp.float32) + partner_grad.astype(jnp.float32)) * 0.5
    momentum_f = (
        decay_old * momentum.astype(jnp.float32)
        - grad_rate * mean_grad
        - pull_rate * (weights_f32 - mean_weights)
    )
    new_weights = weights_f32 + decay_old * momentum_f - grad_rate * mean_grad
    return new_weights.astype(jnp.bfloat16), momentum_f.astype(jnp.bfloat16)


def spread(array):
    columns = lax.axis_size("column")
    pieces = array.reshape(columns, array.shape[0] // columns, array.shape[1])
    return lax.all_to_all(pieces, "column", split_axis=0, concat_axis=0, tiled=True)


def take(array, index):
    return array.at[index].get(mode="promise_in_bounds")


def cross(pieces, send_index, slots):
    packed = take(pieces, send_index)
    up = lax.ppermute(packed[:slots], "layer", [(i, (i + 1) % LAYERS) for i in range(LAYERS)])
    down = lax.ppermute(packed[slots:], "layer", [(i, (i + 2) % LAYERS) for i in range(LAYERS)])
    return jnp.concatenate([pieces, up, down], axis=0)


def deliver(held, take_index):
    routed = take(held, take_index)
    arrived = lax.all_to_all(routed, "column", split_axis=0, concat_axis=0, tiled=True)
    return arrived.reshape(-1, arrived.shape[-1])


def routes(target, rank, layer, slots):
    columns = target.shape[0]
    ids = jnp.arange(columns, dtype=jnp.int32)
    shift = (jnp.take(target, layer, axis=1) - layer + LAYERS) % LAYERS
    mine_rank = jnp.take(rank, layer, axis=1)
    slot = jnp.where((shift > 0) & (mine_rank < slots), (shift - 1) * slots + mine_rank, -1)
    chosen = slot[None, :] == jnp.arange(2 * slots, dtype=jnp.int32)[:, None]
    send_index = jnp.sum(jnp.where(chosen, ids[None, :], 0), axis=1)
    source = jnp.take(target, layer, axis=1)
    came = (layer - source + LAYERS * columns) % LAYERS
    source_rank = jnp.minimum(jnp.take(rank.reshape(-1), source, axis=0), slots - 1)
    take_index = jnp.where(
        came == 0, source // LAYERS, columns + (came - 1) * slots + source_rank
    )
    return send_index, take_index


def on_device(weights, pseudo_grad, momentum, partner, activations, key_cotangent):
    columns = lax.axis_size("column")
    layer = lax.axis_index("layer")
    weights, pseudo_grad, momentum = weights[0], pseudo_grad[0], momentum[0]

    target = partner.reshape(columns, LAYERS)
    to_layer = (target % LAYERS)[:, :, None] == jnp.arange(LAYERS, dtype=jnp.int32)
    before = jnp.tril(jnp.ones((columns, columns), jnp.int32), -1)
    earlier = jnp.sum(before[:, :, None, None] * to_layer[None].astype(jnp.int32), axis=1)
    rank = jnp.sum(jnp.where(to_layer, earlier, 0), axis=2)
    own = to_layer & (jnp.arange(LAYERS)[None, :, None] == jnp.arange(LAYERS)[None, None, :])
    crowded = jnp.max(jnp.where(jnp.any(own, axis=2), 0, rank)) >= SLOTS

    gathered = lax.all_gather(key_cotangent, "fsdp", axis=0, tiled=True)
    send_index, take_index = routes(target, rank, layer, SLOTS)
    spread_weights = spread(weights)
    spread_grad = spread(pseudo_grad)
    held_weights = cross(spread_weights, send_index, SLOTS)
    held_grad = cross(spread_grad, send_index, SLOTS)
    held_grad, gathered = lax.optimization_barrier((held_grad, gathered))
    partner_weights = deliver(held_weights, take_index)
    partner_grad = deliver(held_grad, take_index)

    def as_arrived():
        return outer_step(weights, pseudo_grad, momentum, partner_weights, partner_grad)

    def again():
        send_all, take_all = routes(target, rank, layer, columns)
        return outer_step(
            weights,
            pseudo_grad,
            momentum,
            deliver(cross(spread_weights, send_all, columns), take_all),
            deliver(cross(spread_grad, send_all, columns), take_all),
        )

    new_weights, new_momentum = lax.cond(crowded, again, as_arrived)

    contract = (((0,), (0,)), ((), ()))
    grad_f32 = lax.dot_general(activations, gathered, contract, preferred_element_type=jnp.float32)
    weight_grad = grad_f32.astype(jnp.bfloat16)
    return (new_weights[None], new_momentum[None], weight_grad[None])


def solution(mesh):
    replicas, shards = mesh.devices.shape
    grid = Mesh(
        mesh.devices.reshape(replicas // LAYERS, LAYERS, shards), ("column", "layer", "fsdp")
    )
    replica = ("column", "layer")
    block = P(replica, "fsdp", None)
    return jax.shard_map(
        on_device,
        mesh=grid,
        in_specs=(
            block,
            block,
            block,
            P(),
            P(replica, "fsdp"),
            P(("column", "layer", "fsdp"), None),
        ),
        out_specs=(block, block, block),
        check_vma=False,
    )
```

```python
import jax
import jax.numpy as jnp
from jax import lax
from jax.sharding import PartitionSpec as P

UNIT_ROWS = 4
UNIT_COLS = 128

decay_old = 0.5
grad_rate = 0.7
pull_rate = 0.9


def to_pieces(first, second, count):
    rows, cols = first.shape
    quads = [a.reshape(rows // UNIT_ROWS, UNIT_ROWS, cols) for a in (first, second)]
    wide = cols // UNIT_COLS
    per_piece = -(-2 * rows // UNIT_ROWS * wide // count)
    spare = (per_piece * count - 2 * rows // UNIT_ROWS * wide) // wide
    joined = jnp.concatenate([*quads, jnp.zeros((spare, UNIT_ROWS, cols), first.dtype)], axis=0)
    cut = joined.reshape(-1, UNIT_ROWS, wide, UNIT_COLS).transpose(0, 2, 1, 3)
    return cut.reshape(count, per_piece, UNIT_ROWS, UNIT_COLS)


def from_pieces(pieces, rows, cols):
    wide = cols // UNIT_COLS
    cut = pieces.reshape(-1, wide, UNIT_ROWS, UNIT_COLS)
    quads = rows // UNIT_ROWS
    parts = (cut[:quads], cut[quads : 2 * quads])
    return [p.transpose(0, 2, 1, 3).reshape(rows, cols) for p in parts]


def exchange(pieces):
    return lax.all_to_all(pieces, "replica", split_axis=0, concat_axis=0, tiled=True)


def on_device(weights, pseudo_grad, momentum, partner, activations, key_cotangent):
    replicas = lax.axis_size("replica")
    weights, pseudo_grad, momentum = weights[0], pseudo_grad[0], momentum[0]
    rows, cols = weights.shape
    gathered = lax.all_gather(key_cotangent, "fsdp", axis=0, tiled=True)

    pieces = exchange(to_pieces(weights, pseudo_grad, replicas))
    routed = pieces.at[partner].get(mode="promise_in_bounds")
    routed, gathered = lax.optimization_barrier((routed, gathered))
    partner_weights, partner_grad = lax.optimization_barrier(
        from_pieces(exchange(routed), rows, cols)
    )

    weights_f32 = weights.astype(jnp.float32)
    mean_weights = (weights_f32 + partner_weights.astype(jnp.float32)) * 0.5
    mean_grad = (pseudo_grad.astype(jnp.float32) + partner_grad.astype(jnp.float32)) * 0.5
    momentum_f = (
        decay_old * momentum.astype(jnp.float32)
        - grad_rate * mean_grad
        - pull_rate * (weights_f32 - mean_weights)
    )
    new_weights = weights_f32 + decay_old * momentum_f - grad_rate * mean_grad
    new_weights = new_weights.astype(jnp.bfloat16)
    new_momentum = momentum_f.astype(jnp.bfloat16)

    contract = (((0,), (0,)), ((), ()))
    grad_f32 = lax.dot_general(activations, gathered, contract, preferred_element_type=jnp.float32)
    weight_grad = grad_f32.astype(jnp.bfloat16)
    return (new_weights[None], new_momentum[None], weight_grad[None])


def solution(mesh):
    block = P("replica", "fsdp", None)
    return jax.shard_map(
        on_device,
        mesh=mesh,
        in_specs=(
            block,
            block,
            block,
            P(),
            P("replica", "fsdp"),
            P(("replica", "fsdp"), None),
        ),
        out_specs=(block, block, block),
        check_vma=False,
    )
```

```python
import jax
import jax.numpy as jnp
from jax import lax
from jax.sharding import PartitionSpec as P

UNIT_ROWS = 4
UNIT_COLS = 128

decay_old = 0.5
grad_rate = 0.7
pull_rate = 0.9


def to_pieces(first, second, count):
    rows, cols = first.shape
    quads = [a.reshape(rows // UNIT_ROWS, UNIT_ROWS, cols) for a in (first, second)]
    wide = cols // UNIT_COLS
    per_piece = -(-2 * rows // UNIT_ROWS * wide // count)
    spare = (per_piece * count - 2 * rows // UNIT_ROWS * wide) // wide
    joined = jnp.concatenate([*quads, jnp.zeros((spare, UNIT_ROWS, cols), first.dtype)], axis=0)
    cut = joined.reshape(-1, UNIT_ROWS, wide, UNIT_COLS).transpose(0, 2, 1, 3)
    return cut.reshape(count, per_piece, UNIT_ROWS, UNIT_COLS)


def from_pieces(pieces, rows, cols):
    wide = cols // UNIT_COLS
    cut = pieces.reshape(-1, wide, UNIT_ROWS, UNIT_COLS)
    quads = rows // UNIT_ROWS
    parts = (cut[:quads], cut[quads : 2 * quads])
    return [p.transpose(0, 2, 1, 3).reshape(rows, cols) for p in parts]


def exchange(pieces):
    return lax.all_to_all(pieces, "replica", split_axis=0, concat_axis=0, tiled=True)


def on_device(weights, pseudo_grad, momentum, partner, activations, key_cotangent):
    replicas = lax.axis_size("replica")
    weights, pseudo_grad, momentum = weights[0], pseudo_grad[0], momentum[0]
    rows, cols = weights.shape
    gathered = lax.all_gather(key_cotangent, "fsdp", axis=0, tiled=True)

    pieces = exchange(to_pieces(weights, pseudo_grad, replicas))
    routed = pieces.at[partner].get(mode="promise_in_bounds")
    partner_weights, partner_grad = lax.optimization_barrier(
        from_pieces(exchange(routed), rows, cols)
    )

    weights_f32 = weights.astype(jnp.float32)
    mean_weights = (weights_f32 + partner_weights.astype(jnp.float32)) * 0.5
    mean_grad = (pseudo_grad.astype(jnp.float32) + partner_grad.astype(jnp.float32)) * 0.5
    momentum_f = (
        decay_old * momentum.astype(jnp.float32)
        - grad_rate * mean_grad
        - pull_rate * (weights_f32 - mean_weights)
    )
    new_weights = weights_f32 + decay_old * momentum_f - grad_rate * mean_grad
    new_weights = new_weights.astype(jnp.bfloat16)
    new_momentum = momentum_f.astype(jnp.bfloat16)

    contract = (((0,), (0,)), ((), ()))
    grad_f32 = lax.dot_general(activations, gathered, contract, preferred_element_type=jnp.float32)
    weight_grad = grad_f32.astype(jnp.bfloat16)
    return (new_weights[None], new_momentum[None], weight_grad[None])


def solution(mesh):
    block = P("replica", "fsdp", None)
    return jax.shard_map(
        on_device,
        mesh=mesh,
        in_specs=(
            block,
            block,
            block,
            P(),
            P("replica", "fsdp"),
            P(("replica", "fsdp"), None),
        ),
        out_specs=(block, block, block),
        check_vma=False,
    )
```

```python
import jax
import jax.numpy as jnp
from jax import lax
from jax.sharding import PartitionSpec as P

UNIT_ROWS = 4
UNIT_COLS = 128
CORES = 2

decay_old = 0.5
grad_rate = 0.7
pull_rate = 0.9


def to_pieces(first, second, count):
    rows, cols = first.shape
    quads = [a.reshape(rows // UNIT_ROWS, UNIT_ROWS, cols) for a in (first, second)]
    wide = cols // UNIT_COLS
    per_piece = -(-2 * rows // UNIT_ROWS * wide // count)
    spare = (per_piece * count - 2 * rows // UNIT_ROWS * wide) // wide
    joined = jnp.concatenate([*quads, jnp.zeros((spare, UNIT_ROWS, cols), first.dtype)], axis=0)
    cut = joined.reshape(-1, UNIT_ROWS, wide, UNIT_COLS).transpose(0, 2, 1, 3)
    return cut.reshape(count, per_piece, UNIT_ROWS, UNIT_COLS)


def from_pieces(pieces, rows, cols):
    wide = cols // UNIT_COLS
    cut = pieces.reshape(-1, wide, UNIT_ROWS, UNIT_COLS)
    quads = rows // UNIT_ROWS
    parts = (cut[:quads], cut[quads : 2 * quads])
    return [p.transpose(0, 2, 1, 3).reshape(rows, cols) for p in parts]


def exchange(pieces):
    return lax.all_to_all(pieces, "replica", split_axis=0, concat_axis=0, tiled=True)


def same_core_shards(shard):
    chips = lax.axis_size("fsdp") // CORES
    here = lax.axis_index("fsdp") // CORES
    arrived = [shard]
    for shift in range(1, chips):
        pairs = [
            (chip * CORES + core, (chip + shift) % chips * CORES + core)
            for chip in range(chips)
            for core in range(CORES)
        ]
        arrived.append(lax.ppermute(shard, "fsdp", pairs))
    order = (here - jnp.arange(chips, dtype=jnp.int32) + chips) % chips
    return jnp.stack(arrived), order


def both_cores_shards(arrived, order):
    ordered = arrived.at[order].get(mode="promise_in_bounds")
    shards = lax.axis_size("fsdp")
    swap = [(i, i ^ 1) for i in range(shards)]
    other = lax.ppermute(ordered, "fsdp", swap)
    first = lax.axis_index("fsdp") % CORES == 0
    pair = (jnp.where(first, ordered, other), jnp.where(first, other, ordered))
    return jnp.stack(pair, axis=1).reshape(-1, arrived.shape[-1])


def on_device(weights, pseudo_grad, momentum, partner, activations, key_cotangent):
    replicas = lax.axis_size("replica")
    weights, pseudo_grad, momentum = weights[0], pseudo_grad[0], momentum[0]
    rows, cols = weights.shape

    pieces = exchange(to_pieces(weights, pseudo_grad, replicas))
    routed = pieces.at[partner].get(mode="promise_in_bounds")
    arrived, order = same_core_shards(key_cotangent)
    routed, arrived = lax.optimization_barrier((routed, arrived))
    partner_weights, partner_grad = lax.optimization_barrier(
        from_pieces(exchange(routed), rows, cols)
    )

    weights_f32 = weights.astype(jnp.float32)
    mean_weights = (weights_f32 + partner_weights.astype(jnp.float32)) * 0.5
    mean_grad = (pseudo_grad.astype(jnp.float32) + partner_grad.astype(jnp.float32)) * 0.5
    momentum_f = (
        decay_old * momentum.astype(jnp.float32)
        - grad_rate * mean_grad
        - pull_rate * (weights_f32 - mean_weights)
    )
    new_weights = weights_f32 + decay_old * momentum_f - grad_rate * mean_grad
    new_weights = new_weights.astype(jnp.bfloat16)
    new_momentum = momentum_f.astype(jnp.bfloat16)

    gathered = both_cores_shards(arrived, order)
    contract = (((0,), (0,)), ((), ()))
    grad_f32 = lax.dot_general(activations, gathered, contract, preferred_element_type=jnp.float32)
    weight_grad = grad_f32.astype(jnp.bfloat16)
    return (new_weights[None], new_momentum[None], weight_grad[None])


def solution(mesh):
    block = P("replica", "fsdp", None)
    return jax.shard_map(
        on_device,
        mesh=mesh,
        in_specs=(
            block,
            block,
            block,
            P(),
            P("replica", "fsdp"),
            P(("replica", "fsdp"), None),
        ),
        out_specs=(block, block, block),
        check_vma=False,
    )
```

```python
import jax
import jax.numpy as jnp
from jax import lax
from jax.sharding import PartitionSpec as P

UNIT_ROWS = 4
UNIT_COLS = 128
CORES = 2

decay_old = 0.5
grad_rate = 0.7
pull_rate = 0.9


def to_pieces(first, second, count):
    rows, cols = first.shape
    quads = [a.reshape(rows // UNIT_ROWS, UNIT_ROWS, cols) for a in (first, second)]
    wide = cols // UNIT_COLS
    per_piece = -(-2 * rows // UNIT_ROWS * wide // count)
    spare = (per_piece * count - 2 * rows // UNIT_ROWS * wide) // wide
    joined = jnp.concatenate([*quads, jnp.zeros((spare, UNIT_ROWS, cols), first.dtype)], axis=0)
    cut = joined.reshape(-1, UNIT_ROWS, wide, UNIT_COLS).transpose(0, 2, 1, 3)
    return cut.reshape(count, per_piece, UNIT_ROWS, UNIT_COLS)


def from_pieces(pieces, rows, cols):
    wide = cols // UNIT_COLS
    cut = pieces.reshape(-1, wide, UNIT_ROWS, UNIT_COLS)
    quads = rows // UNIT_ROWS
    parts = (cut[:quads], cut[quads : 2 * quads])
    return [p.transpose(0, 2, 1, 3).reshape(rows, cols) for p in parts]


def exchange(pieces):
    return lax.all_to_all(pieces, "replica", split_axis=0, concat_axis=0, tiled=True)


def core_pairs(chips, shifts):
    return [
        (chip * CORES + core, (chip + shifts[core]) % chips * CORES + core)
        for chip in range(chips)
        for core in range(CORES)
    ]


def by_core(mine, other):
    first = lax.axis_index("fsdp") % CORES == 0
    return jnp.where(first, mine, other), jnp.where(first, other, mine)


def swap_cores(array):
    return lax.ppermute(array, "fsdp", [(i, i ^ 1) for i in range(lax.axis_size("fsdp"))])


def chips_shards(shard):
    chips = lax.axis_size("fsdp") // CORES
    far = lax.ppermute(shard, "fsdp", core_pairs(chips, (2, 2)))
    chip = jnp.concatenate(by_core(shard, swap_cores(shard)), axis=0)
    near = lax.ppermute(chip, "fsdp", core_pairs(chips, (1, chips - 1)))
    return chip, jnp.concatenate([near, far], axis=0)


def all_shards(chip, fetched):
    tokens = chip.shape[0]
    chips = lax.axis_size("fsdp") // CORES
    here = lax.axis_index("fsdp") // CORES
    even, odd = by_core(fetched, swap_cores(fetched))
    blocks = (chip, even[:tokens], jnp.concatenate([even[tokens:], odd[tokens:]]), odd[:tokens])
    order = (here - jnp.arange(chips, dtype=jnp.int32) + chips) % chips
    ordered = jnp.stack(blocks).at[order].get(mode="promise_in_bounds")
    return ordered.reshape(-1, chip.shape[-1])


def on_device(weights, pseudo_grad, momentum, partner, activations, key_cotangent):
    replicas = lax.axis_size("replica")
    weights, pseudo_grad, momentum = weights[0], pseudo_grad[0], momentum[0]
    rows, cols = weights.shape

    pieces = exchange(to_pieces(weights, pseudo_grad, replicas))
    routed = pieces.at[partner].get(mode="promise_in_bounds")
    chip, fetched = chips_shards(key_cotangent)
    routed, fetched = lax.optimization_barrier((routed, fetched))
    partner_weights, partner_grad = lax.optimization_barrier(
        from_pieces(exchange(routed), rows, cols)
    )

    weights_f32 = weights.astype(jnp.float32)
    mean_weights = (weights_f32 + partner_weights.astype(jnp.float32)) * 0.5
    mean_grad = (pseudo_grad.astype(jnp.float32) + partner_grad.astype(jnp.float32)) * 0.5
    momentum_f = (
        decay_old * momentum.astype(jnp.float32)
        - grad_rate * mean_grad
        - pull_rate * (weights_f32 - mean_weights)
    )
    new_weights = weights_f32 + decay_old * momentum_f - grad_rate * mean_grad
    new_weights = new_weights.astype(jnp.bfloat16)
    new_momentum = momentum_f.astype(jnp.bfloat16)

    gathered = all_shards(chip, fetched)
    contract = (((0,), (0,)), ((), ()))
    grad_f32 = lax.dot_general(activations, gathered, contract, preferred_element_type=jnp.float32)
    weight_grad = grad_f32.astype(jnp.bfloat16)
    return (new_weights[None], new_momentum[None], weight_grad[None])


def solution(mesh):
    block = P("replica", "fsdp", None)
    return jax.shard_map(
        on_device,
        mesh=mesh,
        in_specs=(
            block,
            block,
            block,
            P(),
            P("replica", "fsdp"),
            P(("replica", "fsdp"), None),
        ),
        out_specs=(block, block, block),
        check_vma=False,
    )
```

```python
import jax
import jax.numpy as jnp
from jax import lax
from jax.experimental import pallas as pl
from jax.experimental.pallas import tpu as pltpu
from jax.sharding import PartitionSpec as P

UNIT_ROWS = 4
UNIT_COLS = 128
CORES = 2

decay_old = 0.5
grad_rate = 0.7
pull_rate = 0.9


def to_pieces(first, second, count):
    rows, cols = first.shape
    quads = [a.reshape(rows // UNIT_ROWS, UNIT_ROWS, cols) for a in (first, second)]
    wide = cols // UNIT_COLS
    per_piece = -(-2 * rows // UNIT_ROWS * wide // count)
    spare = (per_piece * count - 2 * rows // UNIT_ROWS * wide) // wide
    total = 2 * rows // UNIT_ROWS + spare
    joined = jnp.zeros((total, UNIT_ROWS, cols), first.dtype)
    for i, q in enumerate(quads):
        joined = lax.dynamic_update_slice(joined, q, (i * rows // UNIT_ROWS, 0, 0))
    cut = joined.reshape(-1, UNIT_ROWS, wide, UNIT_COLS).transpose(0, 2, 1, 3)
    return cut.reshape(count, per_piece, UNIT_ROWS, UNIT_COLS)


def from_pieces(pieces, rows, cols):
    wide = cols // UNIT_COLS
    cut = pieces.reshape(-1, wide, UNIT_ROWS, UNIT_COLS)
    quads = rows // UNIT_ROWS
    parts = (cut[:quads], cut[quads : 2 * quads])
    return [p.transpose(0, 2, 1, 3).reshape(rows, cols) for p in parts]


def exchange(pieces):
    return lax.all_to_all(pieces, "replica", split_axis=0, concat_axis=0, tiled=True)


def route_body(partner_ref, pieces_ref, routed_ref, sem):
    def start(i, carry):
        source = pieces_ref.at[partner_ref[i]]
        pltpu.make_async_copy(source, routed_ref.at[i], sem).start()
        return carry

    lax.fori_loop(0, routed_ref.shape[0], start, 0, unroll=8)
    pltpu.make_async_copy(pieces_ref, routed_ref, sem).wait()


def route(pieces, partner):
    return pl.pallas_call(
        route_body,
        out_shape=jax.ShapeDtypeStruct(pieces.shape, pieces.dtype),
        in_specs=[
            pl.BlockSpec(memory_space=pltpu.SMEM),
            pl.BlockSpec(memory_space=pl.ANY),
        ],
        out_specs=pl.BlockSpec(memory_space=pl.ANY),
        scratch_shapes=[pltpu.SemaphoreType.DMA],
        compiler_params=pltpu.CompilerParams(vmem_limit_bytes=1 << 20),
        cost_estimate=pl.CostEstimate(
            flops=0, bytes_accessed=2 * pieces.size * pieces.dtype.itemsize, transcendentals=0
        ),
    )(partner, pieces)


def core_pairs(chips, shifts):
    return [
        (chip * CORES + core, (chip + shifts[core]) % chips * CORES + core)
        for chip in range(chips)
        for core in range(CORES)
    ]


def by_core(mine, other):
    first = lax.axis_index("fsdp") % CORES == 0
    return jnp.where(first, mine, other), jnp.where(first, other, mine)


def swap_cores(array):
    return lax.ppermute(array, "fsdp", [(i, i ^ 1) for i in range(lax.axis_size("fsdp"))])


def chips_shards(shard):
    chips = lax.axis_size("fsdp") // CORES
    far = lax.ppermute(shard, "fsdp", core_pairs(chips, (2, 2)))
    chip = jnp.concatenate(by_core(shard, swap_cores(shard)), axis=0)
    near = lax.ppermute(chip, "fsdp", core_pairs(chips, (1, chips - 1)))
    return chip, jnp.concatenate([near, far], axis=0)


def all_shards(chip, fetched):
    tokens = chip.shape[0]
    chips = lax.axis_size("fsdp") // CORES
    here = lax.axis_index("fsdp") // CORES
    even, odd = by_core(fetched, swap_cores(fetched))
    blocks = (chip, even[:tokens], jnp.concatenate([even[tokens:], odd[tokens:]]), odd[:tokens])
    order = (here - jnp.arange(chips, dtype=jnp.int32) + chips) % chips
    ordered = jnp.stack(blocks).at[order].get(mode="promise_in_bounds")
    return ordered.reshape(-1, chip.shape[-1])


def on_device(weights, pseudo_grad, momentum, partner, activations, key_cotangent):
    replicas = lax.axis_size("replica")
    weights, pseudo_grad, momentum = weights[0], pseudo_grad[0], momentum[0]
    rows, cols = weights.shape

    pieces = exchange(to_pieces(weights, pseudo_grad, replicas))
    routed = route(pieces, partner)
    chip, fetched = chips_shards(key_cotangent)
    routed, fetched = lax.optimization_barrier((routed, fetched))
    partner_weights, partner_grad = lax.optimization_barrier(
        from_pieces(exchange(routed), rows, cols)
    )

    weights_f32 = weights.astype(jnp.float32)
    mean_weights = (weights_f32 + partner_weights.astype(jnp.float32)) * 0.5
    mean_grad = (pseudo_grad.astype(jnp.float32) + partner_grad.astype(jnp.float32)) * 0.5
    momentum_f = (
        decay_old * momentum.astype(jnp.float32)
        - grad_rate * mean_grad
        - pull_rate * (weights_f32 - mean_weights)
    )
    new_weights = weights_f32 + decay_old * momentum_f - grad_rate * mean_grad
    new_weights = new_weights.astype(jnp.bfloat16)
    new_momentum = momentum_f.astype(jnp.bfloat16)

    gathered = all_shards(chip, fetched)
    contract = (((0,), (0,)), ((), ()))
    grad_f32 = lax.dot_general(activations, gathered, contract, preferred_element_type=jnp.float32)
    weight_grad = grad_f32.astype(jnp.bfloat16)
    return (new_weights[None], new_momentum[None], weight_grad[None])


def solution(mesh):
    block = P("replica", "fsdp", None)
    return jax.shard_map(
        on_device,
        mesh=mesh,
        in_specs=(
            block,
            block,
            block,
            P(),
            P("replica", "fsdp"),
            P(("replica", "fsdp"), None),
        ),
        out_specs=(block, block, block),
        check_vma=False,
    )
```

```python
import jax
import jax.numpy as jnp
from jax import lax
from jax.experimental import pallas as pl
from jax.experimental.pallas import tpu as pltpu
from jax.sharding import Mesh
from jax.sharding import PartitionSpec as P

UNIT_ROWS = 4
UNIT_COLS = 128
CORES = 2
LAYERS = 3
RANKS = ("layer", "column")

decay_old = 0.5
grad_rate = 0.7
pull_rate = 0.9


def join_body(first_ref, second_ref, joined_ref, sems):
    half = first_ref.shape[0]
    spare = joined_ref.shape[0] - 2 * half
    copies = (
        (first_ref, joined_ref.at[pl.ds(0, half)]),
        (second_ref, joined_ref.at[pl.ds(half, half)]),
        (first_ref.at[pl.ds(0, spare)], joined_ref.at[pl.ds(2 * half, spare)]),
    )
    started = [pltpu.make_async_copy(a, b, sems.at[i]) for i, (a, b) in enumerate(copies)]
    for copy in started:
        copy.start()
    for copy in started:
        copy.wait()


def join(first, second, spare):
    shape = (2 * first.shape[0] + spare, *first.shape[1:])
    return pl.pallas_call(
        join_body,
        out_shape=jax.ShapeDtypeStruct(shape, first.dtype),
        in_specs=[pl.BlockSpec(memory_space=pl.ANY)] * 2,
        out_specs=pl.BlockSpec(memory_space=pl.ANY),
        scratch_shapes=[pltpu.SemaphoreType.DMA((3,))],
        compiler_params=pltpu.CompilerParams(vmem_limit_bytes=1 << 20),
    )(first, second)


def to_pieces(first, second, count):
    rows, cols = first.shape
    quads = [a.reshape(rows // UNIT_ROWS, UNIT_ROWS, cols) for a in (first, second)]
    wide = cols // UNIT_COLS
    per_piece = -(-2 * rows // UNIT_ROWS * wide // count)
    spare = (per_piece * count - 2 * rows // UNIT_ROWS * wide) // wide
    joined = join(*quads, spare)
    cut = joined.reshape(-1, UNIT_ROWS, wide, UNIT_COLS).transpose(0, 2, 1, 3)
    return cut.reshape(count, per_piece, UNIT_ROWS, UNIT_COLS)


def from_pieces(pieces, rows, cols):
    wide = cols // UNIT_COLS
    cut = pieces.reshape(-1, wide, UNIT_ROWS, UNIT_COLS)
    quads = rows // UNIT_ROWS
    parts = (cut[:quads], cut[quads : 2 * quads])
    return [p.transpose(0, 2, 1, 3).reshape(rows, cols) for p in parts]


def exchange(pieces):
    return lax.all_to_all(pieces, RANKS, split_axis=0, concat_axis=0, tiled=True)


def route_body(partner_ref, pieces_ref, routed_ref, sem):
    def start(i, carry):
        source = pieces_ref.at[partner_ref[i]]
        pltpu.make_async_copy(source, routed_ref.at[i], sem).start()
        return carry

    lax.fori_loop(0, routed_ref.shape[0], start, 0, unroll=8)
    pltpu.make_async_copy(pieces_ref, routed_ref, sem).wait()


def route(pieces, partner):
    return pl.pallas_call(
        route_body,
        out_shape=jax.ShapeDtypeStruct(pieces.shape, pieces.dtype),
        in_specs=[
            pl.BlockSpec(memory_space=pltpu.SMEM),
            pl.BlockSpec(memory_space=pl.ANY),
        ],
        out_specs=pl.BlockSpec(memory_space=pl.ANY),
        scratch_shapes=[pltpu.SemaphoreType.DMA],
        compiler_params=pltpu.CompilerParams(vmem_limit_bytes=1 << 20),
        cost_estimate=pl.CostEstimate(
            flops=0, bytes_accessed=2 * pieces.size * pieces.dtype.itemsize, transcendentals=0
        ),
    )(partner, pieces)


def core_pairs(chips, shifts):
    return [
        (chip * CORES + core, (chip + shifts[core]) % chips * CORES + core)
        for chip in range(chips)
        for core in range(CORES)
    ]


def by_core(mine, other):
    first = lax.axis_index("fsdp") % CORES == 0
    return jnp.where(first, mine, other), jnp.where(first, other, mine)


def swap_cores(array):
    return lax.ppermute(array, "fsdp", [(i, i ^ 1) for i in range(lax.axis_size("fsdp"))])


def chips_shards(shard):
    chips = lax.axis_size("fsdp") // CORES
    far = lax.ppermute(shard, "fsdp", core_pairs(chips, (2, 2)))
    chip = jnp.concatenate(by_core(shard, swap_cores(shard)), axis=0)
    near = lax.ppermute(chip, "fsdp", core_pairs(chips, (1, chips - 1)))
    return chip, jnp.concatenate([near, far], axis=0)


def all_shards(chip, fetched):
    tokens = chip.shape[0]
    chips = lax.axis_size("fsdp") // CORES
    here = lax.axis_index("fsdp") // CORES
    even, odd = by_core(fetched, swap_cores(fetched))
    blocks = (chip, even[:tokens], jnp.concatenate([even[tokens:], odd[tokens:]]), odd[:tokens])
    order = (here - jnp.arange(chips, dtype=jnp.int32) + chips) % chips
    ordered = jnp.stack(blocks).at[order].get(mode="promise_in_bounds")
    return ordered.reshape(-1, chip.shape[-1])


def on_device(weights, pseudo_grad, momentum, partner, activations, key_cotangent):
    columns = lax.axis_size("column")
    replicas = columns * LAYERS
    weights, pseudo_grad, momentum = weights[0], pseudo_grad[0], momentum[0]
    rows, cols = weights.shape

    pieces = exchange(to_pieces(weights, pseudo_grad, replicas))
    by_rank = partner.reshape(columns, LAYERS).T.reshape(-1)
    routed = route(pieces, by_rank % LAYERS * columns + by_rank // LAYERS)
    chip, fetched = chips_shards(key_cotangent)
    routed, fetched = lax.optimization_barrier((routed, fetched))
    partner_weights, partner_grad = lax.optimization_barrier(
        from_pieces(exchange(routed), rows, cols)
    )

    weights_f32 = weights.astype(jnp.float32)
    mean_weights = (weights_f32 + partner_weights.astype(jnp.float32)) * 0.5
    mean_grad = (pseudo_grad.astype(jnp.float32) + partner_grad.astype(jnp.float32)) * 0.5
    momentum_f = (
        decay_old * momentum.astype(jnp.float32)
        - grad_rate * mean_grad
        - pull_rate * (weights_f32 - mean_weights)
    )
    new_weights = weights_f32 + decay_old * momentum_f - grad_rate * mean_grad
    new_weights = new_weights.astype(jnp.bfloat16)
    new_momentum = momentum_f.astype(jnp.bfloat16)

    gathered = all_shards(chip, fetched)
    contract = (((0,), (0,)), ((), ()))
    grad_f32 = lax.dot_general(activations, gathered, contract, preferred_element_type=jnp.float32)
    weight_grad = grad_f32.astype(jnp.bfloat16)
    return (new_weights[None], new_momentum[None], weight_grad[None])


def solution(mesh):
    replicas, shards = mesh.devices.shape
    grid = Mesh(
        mesh.devices.reshape(replicas // LAYERS, LAYERS, shards), ("column", "layer", "fsdp")
    )
    replica = ("column", "layer")
    block = P(replica, "fsdp", None)
    return jax.shard_map(
        on_device,
        mesh=grid,
        in_specs=(
            block,
            block,
            block,
            P(),
            P(replica, "fsdp"),
            P(("column", "layer", "fsdp"), None),
        ),
        out_specs=(block, block, block),
        check_vma=False,
    )
```

```python
import jax
import jax.numpy as jnp
from jax import lax
from jax.experimental import pallas as pl
from jax.experimental.pallas import tpu as pltpu
from jax.sharding import Mesh
from jax.sharding import PartitionSpec as P

UNIT_ROWS = 4
UNIT_COLS = 128
CORES = 2
LAYERS = 3
RANKS = ("layer", "column")

decay_old = 0.5
grad_rate = 0.7
pull_rate = 0.9


def join_body(first_ref, second_ref, joined_ref, sems):
    half = first_ref.shape[0]
    spare = joined_ref.shape[0] - 2 * half
    copies = (
        (first_ref, joined_ref.at[pl.ds(0, half)]),
        (second_ref, joined_ref.at[pl.ds(half, half)]),
        (first_ref.at[pl.ds(0, spare)], joined_ref.at[pl.ds(2 * half, spare)]),
    )
    started = [pltpu.make_async_copy(a, b, sems.at[i]) for i, (a, b) in enumerate(copies)]
    for copy in started:
        copy.start()
    for copy in started:
        copy.wait()


def join(first, second, spare):
    shape = (2 * first.shape[0] + spare, *first.shape[1:])
    return pl.pallas_call(
        join_body,
        out_shape=jax.ShapeDtypeStruct(shape, first.dtype),
        in_specs=[pl.BlockSpec(memory_space=pl.ANY)] * 2,
        out_specs=pl.BlockSpec(memory_space=pl.ANY),
        scratch_shapes=[pltpu.SemaphoreType.DMA((3,))],
        compiler_params=pltpu.CompilerParams(vmem_limit_bytes=1 << 20),
    )(first, second)


def to_pieces(first, second, count):
    rows, cols = first.shape
    quads = [a.reshape(rows // UNIT_ROWS, UNIT_ROWS, cols) for a in (first, second)]
    wide = cols // UNIT_COLS
    per_piece = -(-2 * rows // UNIT_ROWS * wide // count)
    spare = (per_piece * count - 2 * rows // UNIT_ROWS * wide) // wide
    joined = join(*quads, spare)
    cut = joined.reshape(-1, UNIT_ROWS, wide, UNIT_COLS).transpose(0, 2, 1, 3)
    return cut.reshape(count, per_piece, UNIT_ROWS, UNIT_COLS)


def from_pieces(pieces, rows, cols):
    wide = cols // UNIT_COLS
    cut = pieces.reshape(-1, wide, UNIT_ROWS, UNIT_COLS)
    quads = rows // UNIT_ROWS
    parts = (cut[:quads], cut[quads : 2 * quads])
    return [p.transpose(0, 2, 1, 3).reshape(rows, cols) for p in parts]


def exchange(pieces):
    return lax.all_to_all(pieces, RANKS, split_axis=0, concat_axis=0, tiled=True)


def route_body(partner_ref, pieces_ref, routed_ref, sem):
    def start(i, carry):
        source = pieces_ref.at[partner_ref[i]]
        pltpu.make_async_copy(source, routed_ref.at[i], sem).start()
        return carry

    lax.fori_loop(0, routed_ref.shape[0], start, 0, unroll=8)
    pltpu.make_async_copy(pieces_ref, routed_ref, sem).wait()


def route(pieces, partner):
    return pl.pallas_call(
        route_body,
        out_shape=jax.ShapeDtypeStruct(pieces.shape, pieces.dtype),
        in_specs=[
            pl.BlockSpec(memory_space=pltpu.SMEM),
            pl.BlockSpec(memory_space=pl.ANY),
        ],
        out_specs=pl.BlockSpec(memory_space=pl.ANY),
        scratch_shapes=[pltpu.SemaphoreType.DMA],
        compiler_params=pltpu.CompilerParams(vmem_limit_bytes=1 << 20),
        cost_estimate=pl.CostEstimate(
            flops=0, bytes_accessed=2 * pieces.size * pieces.dtype.itemsize, transcendentals=0
        ),
    )(partner, pieces)


def core_pairs(chips, shifts):
    return [
        (chip * CORES + core, (chip + shifts[core]) % chips * CORES + core)
        for chip in range(chips)
        for core in range(CORES)
    ]


def by_core(mine, other):
    first = lax.axis_index("fsdp") % CORES == 0
    return jnp.where(first, mine, other), jnp.where(first, other, mine)


def swap_cores(array):
    return lax.ppermute(array, "fsdp", [(i, i ^ 1) for i in range(lax.axis_size("fsdp"))])


def near_shards(shard):
    chips = lax.axis_size("fsdp") // CORES
    chip = jnp.concatenate(by_core(shard, swap_cores(shard)), axis=0)
    return chip, lax.ppermute(chip, "fsdp", core_pairs(chips, (1, chips - 1)))


def all_shards(chip, near):
    tokens = chip.shape[0]
    chips = lax.axis_size("fsdp") // CORES
    here = lax.axis_index("fsdp") // CORES
    own_core = by_core(near[: tokens // CORES], near[tokens // CORES :])[0]
    far = lax.ppermute(own_core, "fsdp", core_pairs(chips, (1, chips - 1)))
    fetched = jnp.concatenate([near, far], axis=0)
    even, odd = by_core(fetched, swap_cores(fetched))
    blocks = (chip, even[:tokens], jnp.concatenate([even[tokens:], odd[tokens:]]), odd[:tokens])
    order = (here - jnp.arange(chips, dtype=jnp.int32) + chips) % chips
    ordered = jnp.stack(blocks).at[order].get(mode="promise_in_bounds")
    return ordered.reshape(-1, chip.shape[-1])


def on_device(weights, pseudo_grad, momentum, partner, activations, key_cotangent):
    columns = lax.axis_size("column")
    replicas = columns * LAYERS
    weights, pseudo_grad, momentum = weights[0], pseudo_grad[0], momentum[0]
    rows, cols = weights.shape

    pieces = exchange(to_pieces(weights, pseudo_grad, replicas))
    by_rank = partner.reshape(columns, LAYERS).T.reshape(-1)
    routed = route(pieces, by_rank % LAYERS * columns + by_rank // LAYERS)
    chip, near = near_shards(key_cotangent)
    routed, near = lax.optimization_barrier((routed, near))
    partner_weights, partner_grad = lax.optimization_barrier(
        from_pieces(exchange(routed), rows, cols)
    )

    weights_f32 = weights.astype(jnp.float32)
    mean_weights = (weights_f32 + partner_weights.astype(jnp.float32)) * 0.5
    mean_grad = (pseudo_grad.astype(jnp.float32) + partner_grad.astype(jnp.float32)) * 0.5
    momentum_f = (
        decay_old * momentum.astype(jnp.float32)
        - grad_rate * mean_grad
        - pull_rate * (weights_f32 - mean_weights)
    )
    new_weights = weights_f32 + decay_old * momentum_f - grad_rate * mean_grad
    new_weights = new_weights.astype(jnp.bfloat16)
    new_momentum = momentum_f.astype(jnp.bfloat16)

    gathered = all_shards(chip, near)
    contract = (((0,), (0,)), ((), ()))
    grad_f32 = lax.dot_general(activations, gathered, contract, preferred_element_type=jnp.float32)
    weight_grad = grad_f32.astype(jnp.bfloat16)
    return (new_weights[None], new_momentum[None], weight_grad[None])


def solution(mesh):
    replicas, shards = mesh.devices.shape
    grid = Mesh(
        mesh.devices.reshape(replicas // LAYERS, LAYERS, shards), ("column", "layer", "fsdp")
    )
    replica = ("column", "layer")
    block = P(replica, "fsdp", None)
    return jax.shard_map(
        on_device,
        mesh=grid,
        in_specs=(
            block,
            block,
            block,
            P(),
            P(replica, "fsdp"),
            P(("column", "layer", "fsdp"), None),
        ),
        out_specs=(block, block, block),
        check_vma=False,
    )
```

```python
import jax
import jax.numpy as jnp
from jax import lax
from jax.experimental import pallas as pl
from jax.experimental.pallas import tpu as pltpu
from jax.sharding import Mesh
from jax.sharding import PartitionSpec as P

UNIT_ROWS = 4
UNIT_COLS = 128
CORES = 2
LAYERS = 3
RANKS = ("layer", "column")

decay_old = 0.5
grad_rate = 0.7
pull_rate = 0.9


def join_body(first_ref, second_ref, joined_ref, sems):
    half = first_ref.shape[0]
    spare = joined_ref.shape[0] - 2 * half
    copies = (
        (first_ref, joined_ref.at[pl.ds(0, half)]),
        (second_ref, joined_ref.at[pl.ds(half, half)]),
        (first_ref.at[pl.ds(0, spare)], joined_ref.at[pl.ds(2 * half, spare)]),
    )
    started = [pltpu.make_async_copy(a, b, sems.at[i]) for i, (a, b) in enumerate(copies)]
    for copy in started:
        copy.start()
    for copy in started:
        copy.wait()


def join(first, second, spare):
    shape = (2 * first.shape[0] + spare, *first.shape[1:])
    return pl.pallas_call(
        join_body,
        out_shape=jax.ShapeDtypeStruct(shape, first.dtype),
        in_specs=[pl.BlockSpec(memory_space=pl.ANY)] * 2,
        out_specs=pl.BlockSpec(memory_space=pl.ANY),
        scratch_shapes=[pltpu.SemaphoreType.DMA((3,))],
        compiler_params=pltpu.CompilerParams(vmem_limit_bytes=1 << 20),
    )(first, second)


def to_pieces(first, second, count):
    rows, cols = first.shape
    quads = [a.reshape(rows // UNIT_ROWS, UNIT_ROWS, cols) for a in (first, second)]
    wide = cols // UNIT_COLS
    per_piece = -(-2 * rows // UNIT_ROWS * wide // count)
    spare = (per_piece * count - 2 * rows // UNIT_ROWS * wide) // wide
    joined = join(*quads, spare)
    cut = joined.reshape(-1, UNIT_ROWS, wide, UNIT_COLS).transpose(0, 2, 1, 3)
    return cut.reshape(count, per_piece, UNIT_ROWS, UNIT_COLS)


def from_pieces(pieces, rows, cols):
    wide = cols // UNIT_COLS
    cut = pieces.reshape(-1, wide, UNIT_ROWS, UNIT_COLS)
    quads = rows // UNIT_ROWS
    parts = (cut[:quads], cut[quads : 2 * quads])
    return [p.transpose(0, 2, 1, 3).reshape(rows, cols) for p in parts]


def exchange(pieces):
    return lax.all_to_all(pieces, RANKS, split_axis=0, concat_axis=0, tiled=True)


def route_body(partner_ref, pieces_ref, routed_ref, sem):
    def start(i, carry):
        source = pieces_ref.at[partner_ref[i]]
        pltpu.make_async_copy(source, routed_ref.at[i], sem).start()
        return carry

    lax.fori_loop(0, routed_ref.shape[0], start, 0, unroll=8)
    pltpu.make_async_copy(pieces_ref, routed_ref, sem).wait()


def route(pieces, partner):
    return pl.pallas_call(
        route_body,
        out_shape=jax.ShapeDtypeStruct(pieces.shape, pieces.dtype),
        in_specs=[
            pl.BlockSpec(memory_space=pltpu.SMEM),
            pl.BlockSpec(memory_space=pl.ANY),
        ],
        out_specs=pl.BlockSpec(memory_space=pl.ANY),
        scratch_shapes=[pltpu.SemaphoreType.DMA],
        compiler_params=pltpu.CompilerParams(vmem_limit_bytes=1 << 20),
        cost_estimate=pl.CostEstimate(
            flops=0, bytes_accessed=2 * pieces.size * pieces.dtype.itemsize, transcendentals=0
        ),
    )(partner, pieces)


def core_pairs(chips, shifts):
    return [
        (chip * CORES + core, (chip + shifts[core]) % chips * CORES + core)
        for chip in range(chips)
        for core in range(CORES)
    ]


def by_core(mine, other):
    first = lax.axis_index("fsdp") % CORES == 0
    return jnp.where(first, mine, other), jnp.where(first, other, mine)


def swap_cores(array):
    return lax.ppermute(array, "fsdp", [(i, i ^ 1) for i in range(lax.axis_size("fsdp"))])


def near_shards(shard):
    chips = lax.axis_size("fsdp") // CORES
    chip = jnp.concatenate(by_core(shard, swap_cores(shard)), axis=0)
    return chip, lax.ppermute(chip, "fsdp", core_pairs(chips, (1, chips - 1)))


def all_shards(chip, near):
    tokens = chip.shape[0]
    chips = lax.axis_size("fsdp") // CORES
    own_core = by_core(near[: tokens // CORES], near[tokens // CORES :])[0]
    far = lax.ppermute(own_core, "fsdp", core_pairs(chips, (1, chips - 1)))
    fetched = jnp.concatenate([near, far], axis=0)
    even, odd = by_core(fetched, swap_cores(fetched))
    return jnp.concatenate([chip, even[:tokens], even[tokens:], odd[tokens:], odd[:tokens]])


def in_arrival_order(activations):
    chips = lax.axis_size("fsdp") // CORES
    here = lax.axis_index("fsdp") // CORES
    order = (here - jnp.arange(chips, dtype=jnp.int32) + chips) % chips
    blocks = activations.reshape(chips, -1, activations.shape[-1])
    return blocks.at[order].get(mode="promise_in_bounds").reshape(activations.shape)


def on_device(weights, pseudo_grad, momentum, partner, activations, key_cotangent):
    columns = lax.axis_size("column")
    replicas = columns * LAYERS
    weights, pseudo_grad, momentum = weights[0], pseudo_grad[0], momentum[0]
    rows, cols = weights.shape

    pieces = exchange(to_pieces(weights, pseudo_grad, replicas))
    by_rank = partner.reshape(columns, LAYERS).T.reshape(-1)
    routed = route(pieces, by_rank % LAYERS * columns + by_rank // LAYERS)
    chip, near = near_shards(key_cotangent)
    activations = in_arrival_order(activations)
    routed, near, activations = lax.optimization_barrier((routed, near, activations))
    partner_weights, partner_grad = lax.optimization_barrier(
        from_pieces(exchange(routed), rows, cols)
    )

    weights_f32 = weights.astype(jnp.float32)
    mean_weights = (weights_f32 + partner_weights.astype(jnp.float32)) * 0.5
    mean_grad = (pseudo_grad.astype(jnp.float32) + partner_grad.astype(jnp.float32)) * 0.5
    momentum_f = (
        decay_old * momentum.astype(jnp.float32)
        - grad_rate * mean_grad
        - pull_rate * (weights_f32 - mean_weights)
    )
    new_weights = weights_f32 + decay_old * momentum_f - grad_rate * mean_grad
    new_weights = new_weights.astype(jnp.bfloat16)
    new_momentum = momentum_f.astype(jnp.bfloat16)

    gathered = all_shards(chip, near)
    contract = (((0,), (0,)), ((), ()))
    grad_f32 = lax.dot_general(activations, gathered, contract, preferred_element_type=jnp.float32)
    weight_grad = grad_f32.astype(jnp.bfloat16)
    return (new_weights[None], new_momentum[None], weight_grad[None])


def solution(mesh):
    replicas, shards = mesh.devices.shape
    grid = Mesh(
        mesh.devices.reshape(replicas // LAYERS, LAYERS, shards), ("column", "layer", "fsdp")
    )
    replica = ("column", "layer")
    block = P(replica, "fsdp", None)
    return jax.shard_map(
        on_device,
        mesh=grid,
        in_specs=(
            block,
            block,
            block,
            P(),
            P(replica, "fsdp"),
            P(("column", "layer", "fsdp"), None),
        ),
        out_specs=(block, block, block),
        check_vma=False,
    )
```

```python
import jax
import jax.numpy as jnp
from jax import lax
from jax.experimental import pallas as pl
from jax.experimental.pallas import tpu as pltpu
from jax.sharding import Mesh
from jax.sharding import PartitionSpec as P

UNIT_ROWS = 4
UNIT_COLS = 128
CORES = 2
LAYERS = 3
RANKS = ("layer", "column")

decay_old = 0.5
grad_rate = 0.7
pull_rate = 0.9


def join_body(first_ref, second_ref, joined_ref, sems):
    half = first_ref.shape[0]
    spare = joined_ref.shape[0] - 2 * half
    copies = (
        (first_ref, joined_ref.at[pl.ds(0, half)]),
        (second_ref, joined_ref.at[pl.ds(half, half)]),
        (first_ref.at[pl.ds(0, spare)], joined_ref.at[pl.ds(2 * half, spare)]),
    )
    started = [pltpu.make_async_copy(a, b, sems.at[i]) for i, (a, b) in enumerate(copies)]
    for copy in started:
        copy.start()
    for copy in started:
        copy.wait()


def join(first, second, spare):
    shape = (2 * first.shape[0] + spare, *first.shape[1:])
    return pl.pallas_call(
        join_body,
        out_shape=jax.ShapeDtypeStruct(shape, first.dtype),
        in_specs=[pl.BlockSpec(memory_space=pl.ANY)] * 2,
        out_specs=pl.BlockSpec(memory_space=pl.ANY),
        scratch_shapes=[pltpu.SemaphoreType.DMA((3,))],
        compiler_params=pltpu.CompilerParams(vmem_limit_bytes=1 << 20),
    )(first, second)


def to_pieces(first, second, count):
    rows, cols = first.shape
    quads = [a.reshape(rows // UNIT_ROWS, UNIT_ROWS, cols) for a in (first, second)]
    wide = cols // UNIT_COLS
    per_piece = -(-2 * rows // UNIT_ROWS * wide // count)
    spare = (per_piece * count - 2 * rows // UNIT_ROWS * wide) // wide
    joined = join(*quads, spare)
    cut = joined.reshape(-1, UNIT_ROWS, wide, UNIT_COLS).transpose(0, 2, 1, 3)
    return cut.reshape(count, per_piece, UNIT_ROWS, UNIT_COLS)


def from_pieces(pieces, rows, cols):
    wide = cols // UNIT_COLS
    cut = pieces.reshape(-1, wide, UNIT_ROWS, UNIT_COLS)
    quads = rows // UNIT_ROWS
    parts = (cut[:quads], cut[quads : 2 * quads])
    return [p.transpose(0, 2, 1, 3).reshape(rows, cols) for p in parts]


def exchange(pieces):
    return lax.all_to_all(pieces, RANKS, split_axis=0, concat_axis=0, tiled=True)


def route_body(partner_ref, pieces_ref, routed_ref, sem):
    def start(i, carry):
        source = pieces_ref.at[partner_ref[i]]
        pltpu.make_async_copy(source, routed_ref.at[i], sem).start()
        return carry

    lax.fori_loop(0, routed_ref.shape[0], start, 0, unroll=8)
    pltpu.make_async_copy(pieces_ref, routed_ref, sem).wait()


def route(pieces, partner):
    return pl.pallas_call(
        route_body,
        out_shape=jax.ShapeDtypeStruct(pieces.shape, pieces.dtype),
        in_specs=[
            pl.BlockSpec(memory_space=pltpu.SMEM),
            pl.BlockSpec(memory_space=pl.ANY),
        ],
        out_specs=pl.BlockSpec(memory_space=pl.ANY),
        scratch_shapes=[pltpu.SemaphoreType.DMA],
        compiler_params=pltpu.CompilerParams(vmem_limit_bytes=1 << 20),
        cost_estimate=pl.CostEstimate(
            flops=0, bytes_accessed=2 * pieces.size * pieces.dtype.itemsize, transcendentals=0
        ),
    )(partner, pieces)


def core_pairs(chips, shifts):
    return [
        (chip * CORES + core, (chip + shifts[core]) % chips * CORES + core)
        for chip in range(chips)
        for core in range(CORES)
    ]


def by_core(mine, other):
    first = lax.axis_index("fsdp") % CORES == 0
    return jnp.where(first, mine, other), jnp.where(first, other, mine)


def swap_cores(array):
    return lax.ppermute(array, "fsdp", [(i, i ^ 1) for i in range(lax.axis_size("fsdp"))])


def near_shards(shard):
    chips = lax.axis_size("fsdp") // CORES
    chip = jnp.concatenate(by_core(shard, swap_cores(shard)), axis=0)
    return chip, lax.ppermute(chip, "fsdp", core_pairs(chips, (1, chips - 1)))


def all_shards(chip, near):
    tokens = chip.shape[0]
    chips = lax.axis_size("fsdp") // CORES
    own_core = by_core(near[: tokens // CORES], near[tokens // CORES :])[0]
    far = lax.ppermute(own_core, "fsdp", core_pairs(chips, (1, chips - 1)))
    before, after = by_core(near, swap_cores(near))
    far_even, far_odd = by_core(far, swap_cores(far))
    return jnp.concatenate([chip, before, far_even, far_odd, after])


def in_arrival_order(activations):
    chips = lax.axis_size("fsdp") // CORES
    here = lax.axis_index("fsdp") // CORES
    order = (here - jnp.arange(chips, dtype=jnp.int32) + chips) % chips
    blocks = activations.reshape(chips, -1, activations.shape[-1])
    return blocks.at[order].get(mode="promise_in_bounds").reshape(activations.shape)


def on_device(weights, pseudo_grad, momentum, partner, activations, key_cotangent):
    columns = lax.axis_size("column")
    replicas = columns * LAYERS
    weights, pseudo_grad, momentum = weights[0], pseudo_grad[0], momentum[0]
    rows, cols = weights.shape

    pieces = exchange(to_pieces(weights, pseudo_grad, replicas))
    by_rank = partner.reshape(columns, LAYERS).T.reshape(-1)
    routed = route(pieces, by_rank % LAYERS * columns + by_rank // LAYERS)
    chip, near = near_shards(key_cotangent)
    activations = in_arrival_order(activations)
    routed, near, activations = lax.optimization_barrier((routed, near, activations))
    partner_weights, partner_grad = lax.optimization_barrier(
        from_pieces(exchange(routed), rows, cols)
    )

    weights_f32 = weights.astype(jnp.float32)
    mean_weights = (weights_f32 + partner_weights.astype(jnp.float32)) * 0.5
    mean_grad = (pseudo_grad.astype(jnp.float32) + partner_grad.astype(jnp.float32)) * 0.5
    momentum_f = (
        decay_old * momentum.astype(jnp.float32)
        - grad_rate * mean_grad
        - pull_rate * (weights_f32 - mean_weights)
    )
    new_weights = weights_f32 + decay_old * momentum_f - grad_rate * mean_grad
    new_weights = new_weights.astype(jnp.bfloat16)
    new_momentum = momentum_f.astype(jnp.bfloat16)

    gathered = all_shards(chip, near)
    contract = (((0,), (0,)), ((), ()))
    grad_f32 = lax.dot_general(activations, gathered, contract, preferred_element_type=jnp.float32)
    weight_grad = grad_f32.astype(jnp.bfloat16)
    return (new_weights[None], new_momentum[None], weight_grad[None])


def solution(mesh):
    replicas, shards = mesh.devices.shape
    grid = Mesh(
        mesh.devices.reshape(replicas // LAYERS, LAYERS, shards), ("column", "layer", "fsdp")
    )
    replica = ("column", "layer")
    block = P(replica, "fsdp", None)
    return jax.shard_map(
        on_device,
        mesh=grid,
        in_specs=(
            block,
            block,
            block,
            P(),
            P(replica, "fsdp"),
            P(("column", "layer", "fsdp"), None),
        ),
        out_specs=(block, block, block),
        check_vma=False,
    )
```
